32 devices in a mesh: grp: 2 (over x), rows: 16 (over z, y, core).
Axes of the slice: x: 2, y: 2, z: 4, core: 2. Of those that a mesh axis runs over, the one named last changes fastest.
Arguments:
- histories: float32 [4096, 384], P(('grp', 'rows')), parts along dimension 0, may hold values from -6 to 6
- modal_map: float32 [4096, 8192], P(('grp', 'rows')), parts along dimension 0, may hold values from -0.1875 to 0.1875
- recovery: float32 [8192, 8192], P(('grp', 'rows')), parts along dimension 0, may hold values from -0.0625 to 0.0625
Outputs:
- responses: float32 [8192, 384], P(('grp', 'rows')), parts along dimension 0
- peak_response: float32 [4, 8192], P(None, ('grp', 'rows')), parts along dimension 1
- rms_response: float32 [4, 8192], P(None, ('grp', 'rows')), parts along dimension 1
The draws below stay inside these ranges and needn't reach their ends.
There are 2 independent parts, one for each index of `grp`. The reference program is written for one: setup_inputs(seed, part) draws one part's arguments, and reference() takes and returns one part's arrays. A program takes and returns all parts, laid end to end along the dimension named above; each array names one. Nothing has to cross between parts.
All inputs are finite; a program needn't handle non-finite values.
Results may differ from the reference program's by a relative error of at most 0.000071.
Values sent between devices are 32-bit elements; how exact they have to be, the bound alone decides.
No kernel may reach another device: no remote copies, remote signals or barrier semaphores. Data moves between devices by JAX's collectives and lax.ppermute only.
A program may use at most 64 MiB of HBM per device.

```python
import jax
import jax.numpy as jnp
from jax import lax

MODES = 8192
COUPLED = 2048
CASES = 4
STEPS = 96
OUTPUTS = 4096
TIME = 384


def raised(drawn, stream_key, source, target, parts, factor):
    owner, partner = [(jnp.arange(drawn.shape[axis_at]) // (drawn.shape[axis_at] // parts)).reshape([-1 if axis == axis_at else 1 for axis in range(drawn.ndim)]) for axis_at in (source, target)]
    chosen = jax.random.permutation(stream_key, parts)[partner]
    strong = (owner == chosen) | (owner == (partner + parts // 2) % parts)
    return jnp.where(strong, factor * drawn, drawn)


def block_scale(rng, shape, split, smallest, high):
    factor_of = 1.0
    for dim, shards_of in split:
        draws = jax.random.uniform(jax.random.fold_in(jax.random.fold_in(rng, 6), dim), (shards_of,), jnp.float32, smallest / len(split), high / len(split))
        factor_of = factor_of * jnp.repeat(jnp.exp(draws), shape[dim] // shards_of).reshape((-1,) + (1,) * (len(shape) - 1 - dim))
    return factor_of


def bell_draw(stream_key, shape, spread, most, split=(), held_as=jnp.bfloat16):
    values = jax.random.normal(stream_key, shape, jnp.float32) * spread
    if len(split) > 0:
        values = block_scale(stream_key, shape, split, -0.22, 0.18) * values
    return jnp.clip(values, min=-most, max=most).astype(held_as)


def gaussian_with(own_key, extent, deviation, bound, shards, heavy, dtype=jnp.bfloat16):
    drawn = deviation * jax.random.normal(own_key, extent, jnp.float32)
    if shards:
        drawn = drawn * block_scale(own_key, extent, shards, -0.22, 0.18)
    return jnp.clip(raised(drawn, jax.random.fold_in(own_key, 3), *heavy), -bound, bound).astype(dtype)


def setup_inputs(seed: int = 0, part: int = 0) -> dict:
    streams_of = jax.random.split(jax.random.key(seed), 4)
    part_keys = jax.random.split(jax.random.fold_in(streams_of[3], part), 4)
    return {
        "histories": bell_draw(part_keys[0], (COUPLED, TIME), 1.0, 6.0, ((0, 16),), jnp.float32),
        "modal_map": gaussian_with(part_keys[1], (COUPLED, MODES), COUPLED ** -0.5, 0.1875, ((0, 16),), (0, 1, 16, 2.0), jnp.float32),
        "recovery": bell_draw(part_keys[2], (OUTPUTS, MODES), MODES ** -0.5, 0.0625, ((0, 16),), jnp.float32),
    }


epsilon = 1e-06

def reference(histories, modal_map, recovery):
    modal_rows = lax.dot_general(modal_map, histories, (((0,), (0,)), ((), ())), precision=lax.Precision.HIGHEST, preferred_element_type=jnp.float32)
    responses = jnp.dot(recovery, modal_rows, precision=lax.Precision.HIGHEST, preferred_element_type=jnp.float32)
    by_case = responses.reshape(responses.shape[0], CASES, STEPS)
    peak_response = lax.optimization_barrier(jnp.max(jnp.abs(by_case), axis=2)).T
    rms_response = jnp.sqrt(lax.optimization_barrier(jnp.mean(by_case * by_case, axis=2)) + epsilon).T
    return (responses, peak_response, rms_response)
```

```python
import jax
import jax.numpy as jnp
from jax import lax
from jax.sharding import PartitionSpec as P

CASES = 4
CORES = 2

epsilon = 1e-06


def dot(a, b, a_dim, b_dim):
    return lax.dot_general(
        a,
        b,
        (((a_dim,), (b_dim,)), ((), ())),
        precision=lax.Precision.HIGH,
        preferred_element_type=jnp.float32,
    )


def sizes_of(total, step=128):
    parts = [2, 4, 4, 4, 2]
    if total % (16 * step):
        return [total]
    return [part * (total // 16) for part in parts]


def shards_of(grp, rows):
    sides = 2 if grp == 2 and rows % 4 == 0 else 1
    planes = rows // (sides * CORES)

    def index(z, y, c):
        return (z * sides + y) * CORES + c

    everyone = [(z, y, c) for z in range(planes) for y in range(sides) for c in range(CORES)]
    other_core = [(index(z, y, c), index(z, y, 1 - c)) for z, y, c in everyone]
    other_side = [(index(z, y, c), index(z, 1 - y, c)) for z, y, c in everyone]
    half = planes // 2

    def hop(moves):
        return [(index(z, y, c), index(moves[z], y, c)) for z, y, c in everyone if z in moves]

    inward = [hop({k: k + 1, planes - 1 - k: planes - 2 - k}) for k in range(half - 1)]
    across = hop({half - 1: half, half: half - 1})
    outward = [hop({k + 1: k, planes - 2 - k: planes - 1 - k}) for k in reversed(range(half - 1))]

    def send(value, pairs):
        return lax.ppermute(value, "rows", pairs)

    def shards(histories, modal_map, recovery):
        time_cols = histories.shape[1]
        modes = modal_map.shape[1]
        per_core = modes // CORES
        per_lane = per_core // sides
        place = lax.axis_index("rows")
        core = place % CORES
        side = (place // CORES) % sides
        z = place // (CORES * sides)

        sizes = sizes_of(per_lane)
        offsets = [sum(sizes[:k]) for k in range(len(sizes))]

        def columns(array, at_core, at_side, start, size):
            return lax.dynamic_slice_in_dim(array, at_core * per_core + at_side * per_lane + start, size, 1)

        def of_chip(array, at_side, start, size):
            give = columns(array, 1 - core, at_side, start, size)
            keep = columns(array, core, at_side, start, size)
            return keep, give

        near = [histories]
        if sides == 2:
            near.append(send(histories, other_side))

        def map_piece(start, size):
            kept, given = [], []
            for k in range(sides):
                at_side = side if k == 0 else 1 - side
                keep, give = of_chip(modal_map, at_side, start, size)
                kept.append(keep)
                given.append(columns(modal_map, 1 - core, at_side, start, size))
            got = send(jnp.stack(given), other_core)
            return [jnp.concatenate([kept[k], got[k]]) for k in range(sides)]

        first = map_piece(0, sizes[0])
        rest = map_piece(sizes[0], per_lane - sizes[0]) if len(sizes) > 1 else None

        def map_chunk(i, k):
            if i == 0:
                return first[k]
            return rest[k][:, offsets[i] - sizes[0] : offsets[i] - sizes[0] + sizes[i]]

        far_maps = []
        for i in range(len(sizes)):
            with jax.named_scope(f"far_map_chunk{i}"):
                far_maps.append(send(map_chunk(i, 1), other_side) if sides == 2 else None)
        far = send(jnp.stack(near), other_core)
        histories_here = [jnp.concatenate([near[k], far[k]]) for k in range(sides)]

        steps = len(inward) + 1 + len(outward)
        last = [None]

        def ordered(value):
            if last[0] is None:
                return value
            value, last[0] = lax.optimization_barrier((value, last[0]))
            return value

        held, flying = {}, {}
        recoveries = None
        total = None

        def advance(i, step):
            nonlocal total, recoveries
            if step == 0:
                value = dot(map_chunk(i, 0), histories_here[0], 0, 0)
                if sides == 2:
                    value = value + dot(ordered(far_maps[i]), histories_here[1], 0, 0)
            elif step <= steps:
                got = ordered(flying.pop(i))
                depth = half - 2 - (step - 1 - len(inward) - 1)
                if step - 1 <= len(inward):
                    value = held[i] + got
                else:
                    value = jnp.where((z == depth) | (z == planes - 1 - depth), got, held[i])
            else:
                cut = slice(offsets[i], offsets[i] + sizes[i])
                part = dot(recoveries[0][:, cut], held[i], 1, 0)
                if sides == 2:
                    part = part + dot(recoveries[1][:, cut], ordered(flying.pop(i)), 1, 0)
                total = part if total is None else total + part
                last[0] = total
                return
            held[i] = value
            last[0] = value
            if step < steps:
                flying[i] = send(value, (inward + [across] + outward)[step])
            elif sides == 2:
                flying[i] = send(value, other_side)

        for turn in range(len(sizes) + steps + 1):
            if turn == 2:
                source = ordered(recovery)
                recoveries = []
                for k in range(sides):
                    keep, give = of_chip(source, side if k == 0 else 1 - side, 0, per_lane)
                    recoveries.append(jnp.concatenate([keep, send(columns(source, 1 - core, side if k == 0 else 1 - side, 0, per_lane), other_core)]))
            for step in reversed(range(steps + 2)):
                i = turn - step
                if 0 <= i < len(sizes):
                    with jax.named_scope(f"chunk{i}_step{step}"):
                        advance(i, step)

        mine = recovery.shape[0]
        responses = total[:mine] + send(total[mine:], other_core)
        by_case = responses.reshape(mine, CASES, time_cols // CASES)
        peak_response = jnp.max(jnp.abs(by_case), axis=2).T
        rms_response = jnp.sqrt(jnp.mean(by_case * by_case, axis=2) + epsilon).T
        return (responses, peak_response, rms_response)

    return shards


def solution(mesh):
    return jax.shard_map(
        shards_of(mesh.shape["grp"], mesh.shape["rows"]),
        mesh=mesh,
        in_specs=(P(("grp", "rows"), None), P(("grp", "rows"), None), P(("grp", "rows"), None)),
        out_specs=(P(("grp", "rows"), None), P(None, ("grp", "rows")), P(None, ("grp", "rows"))),
        check_vma=False,
    )
```

```python
import jax
import jax.numpy as jnp
from jax import lax
from jax.experimental import pallas as pl
from jax.experimental.pallas import tpu as pltpu
from jax.sharding import PartitionSpec as P

CASES = 4
CORES = 2
PARTS = [2, 2, 2, 2, 2, 2, 2, 2]
GROUPS = [[0], [1, 2], [3, 4, 5, 6, 7]]
JOINED = []
COSTS = [500000000, 500000000, 500000000, 1, 1, 500000000, 2000000000]
ORDER = "m0 m1 0.0 m2 rs 1.0 rw 0.1 1.1 2.0 0.2 2.1 1.2 0.3 3.0 4.0 2.2 1.3 0.4 3.1 5.0 2.3 1.4 4.1 3.2 6.0 2.4 5.1 4.2 3.3 6.1 7.0 5.2 4.3 3.4 6.2 7.1 5.3 4.4 6.3 7.2 5.4 6.4 7.3 7.4"

epsilon = 1e-06

VMEM = pl.BlockSpec(memory_space=pltpu.VMEM)
ANYWHERE = pl.BlockSpec(memory_space=pl.ANY)


PARAMS = pltpu.CompilerParams(vmem_limit_bytes=16 * 1024 * 1024)


def cost(kind):
    return pl.CostEstimate(flops=COSTS[kind], bytes_accessed=1, transcendentals=0)


def halves(value):
    high = value.astype(jnp.bfloat16)
    return high, (value - high.astype(jnp.float32)).astype(jnp.bfloat16)


def dot(a, b, a_dim):
    a_high, a_low = halves(a)
    b_high, b_low = halves(b)

    def product(x, y):
        return lax.dot_general(x, y, (((a_dim,), (0,)), ((), ())), preferred_element_type=jnp.float32)

    return product(a_high, b_high) + (product(a_high, b_low) + product(a_low, b_high))


def cut_kernel(cuts, at_ref, source, *refs):
    outs, sems = refs[: len(cuts)], refs[len(cuts)]
    copies = []
    for k, (which, begin, size) in enumerate(cuts):
        column = pl.multiple_of(at_ref[which] + begin, 128)
        copies.append(pltpu.make_async_copy(source.at[:, pl.ds(column, size)], outs[k], sems.at[k]))
        copies[-1].start()
    for copy in copies:
        copy.wait()


def cut(source, at, cuts, after=()):
    def kernel(at_ref, source_ref, *refs):
        cut_kernel(cuts, at_ref, source_ref, *refs[len(after) :])

    return pl.pallas_call(
        kernel,
        out_shape=[jax.ShapeDtypeStruct((source.shape[0], size), source.dtype) for _, _, size in cuts],
        in_specs=[pl.BlockSpec(memory_space=pltpu.SMEM), ANYWHERE] + [ANYWHERE] * len(after),
        out_specs=[ANYWHERE] * len(cuts),
        scratch_shapes=[pltpu.SemaphoreType.DMA((len(cuts),))],
        cost_estimate=cost(5),
        compiler_params=PARAMS,
        name="cut_columns",
    )(at, source, *after)


def join(parts, passed, after):
    rows = sum(part.shape[0] for part in parts)
    count = len(parts)

    def kernel(*refs):
        out = refs[count + len(passed) + len(after)]
        begin = 0
        for ref in refs[:count]:
            out[begin : begin + ref.shape[0]] = ref[...]
            begin += ref.shape[0]

    return pl.pallas_call(
        kernel,
        out_shape=[jax.ShapeDtypeStruct((rows, parts[0].shape[1]), jnp.float32)]
        + [jax.ShapeDtypeStruct(piece.shape, piece.dtype) for piece in passed],
        in_specs=[VMEM] * count + [ANYWHERE] * (len(passed) + len(after)),
        out_specs=[VMEM] + [ANYWHERE] * len(passed),
        input_output_aliases={count + k: 1 + k for k in range(len(passed))},
        cost_estimate=cost(6),
        compiler_params=PARAMS,
        name="join",
    )(*parts, *passed, *after)


def plane_sum(at, modal_map, maps, histories, begin, past, size, after):
    count = len(maps) + 1
    pairs = len(histories)
    depth, width = modal_map.shape[0], histories[0].shape[1]

    def kernel(at_ref, *refs):
        sources, history_refs = refs[:count], refs[count : count + pairs]
        out, block, sems = refs[-3:]
        copies = []
        for k in range(count):
            if k == 0:
                source = sources[0].at[:, pl.ds(pl.multiple_of(at_ref[0] + begin, 128), size)]
            else:
                source = sources[k].at[:, pl.ds(past[k - 1], size)]
            copies.append(pltpu.make_async_copy(source, block.at[pl.ds(k * depth, depth)], sems.at[k]))
            copies[-1].start()
        past_block = jnp.concatenate([ref[...] for ref in history_refs])
        for copy in copies:
            copy.wait()
        out[...] = dot(block[...], past_block, 0)

    return pl.pallas_call(
        kernel,
        out_shape=jax.ShapeDtypeStruct((size, width), jnp.float32),
        in_specs=[pl.BlockSpec(memory_space=pltpu.SMEM), ANYWHERE]
        + [ANYWHERE] * len(maps)
        + [VMEM] * pairs
        + [ANYWHERE] * len(after),
        out_specs=VMEM,
        scratch_shapes=[
            pltpu.VMEM((count * depth, size), jnp.float32),
            pltpu.SemaphoreType.DMA((count,)),
        ],
        cost_estimate=cost(0),
        compiler_params=PARAMS,
        name="plane_sum",
    )(at, modal_map, *maps, *histories, *after)


def add(held, got, after):
    def kernel(held_ref, got_ref, *refs):
        refs[-1][...] = held_ref[...] + got_ref[...]

    return pl.pallas_call(
        kernel,
        out_shape=jax.ShapeDtypeStruct(held.shape, held.dtype),
        in_specs=[VMEM, VMEM] + [ANYWHERE] * len(after),
        out_specs=VMEM,
        cost_estimate=cost(1),
        compiler_params=PARAMS,
        name="add",
    )(held, got, *after)


def choose(takes, held, got, before, after):
    above = before.shape[0] if before is not None else 0

    def kernel(takes_ref, held_ref, got_ref, *refs):
        out = refs[-1]
        if above:
            out[:above] = refs[0][...]

        @pl.when(takes_ref[0] == 1)
        def _():
            out[above:] = got_ref[...]

        @pl.when(takes_ref[0] == 0)
        def _():
            out[above:] = held_ref[...]

    return pl.pallas_call(
        kernel,
        out_shape=jax.ShapeDtypeStruct((above + held.shape[0], held.shape[1]), held.dtype),
        in_specs=[pl.BlockSpec(memory_space=pltpu.SMEM), VMEM, VMEM]
        + [VMEM] * (above > 0)
        + [ANYWHERE] * len(after),
        out_specs=VMEM,
        cost_estimate=cost(3),
        compiler_params=PARAMS,
        name="choose",
    )(takes, held, got, *([before] if above else []), *after)


def recover(at, recovery, recovery_got, begin, parts, total, after):
    size = parts[0].shape[0]
    count = len(parts)
    mine = recovery.shape[0]
    has_total = total is not None
    sources = count * 2

    def kernel(at_ref, recovery_ref, got_ref, *refs):
        parts_refs = refs[:count]
        total_ref = refs[count] if has_total else None
        out, block, sems = refs[-3:]
        copies = []
        for k in range(count):
            for j, source in enumerate((recovery_ref, got_ref)):
                column = pl.multiple_of(at_ref[j * count + k] + begin, 128)
                copies.append(
                    pltpu.make_async_copy(
                        source.at[:, pl.ds(column, size)],
                        block.at[pl.ds(j * mine, mine), pl.ds(k * size, size)],
                        sems.at[2 * k + j],
                    )
                )
                copies[-1].start()
        part = jnp.concatenate([ref[...] for ref in parts_refs])
        for copy in copies:
            copy.wait()
        value = dot(block[...], part, 1)
        out[...] = value + total_ref[...] if has_total else value

    rows, columns = 2 * mine, parts[0].shape[1]
    return pl.pallas_call(
        kernel,
        out_shape=jax.ShapeDtypeStruct((rows, columns), jnp.float32),
        in_specs=[pl.BlockSpec(memory_space=pltpu.SMEM), ANYWHERE, ANYWHERE]
        + [VMEM] * count
        + [VMEM] * has_total
        + [ANYWHERE] * len(after),
        out_specs=VMEM,
        scratch_shapes=[pltpu.VMEM((rows, count * size), jnp.float32), pltpu.SemaphoreType.DMA((sources,))],
        cost_estimate=cost(4),
        compiler_params=PARAMS,
        name="recover",
    )(at, recovery, recovery_got, *parts, *([total] if has_total else []), *after)


def finish(responses):
    by_case = responses.reshape(responses.shape[0], CASES, responses.shape[1] // CASES)
    peak_response = jnp.max(jnp.abs(by_case), axis=2).T
    rms_response = jnp.sqrt(jnp.mean(by_case * by_case, axis=2) + epsilon).T
    return (responses, peak_response, rms_response)


def plain(histories, modal_map, recovery):
    modal_rows = lax.psum_scatter(
        lax.dot_general(
            modal_map,
            histories,
            (((0,), (0,)), ((), ())),
            precision=lax.Precision.HIGHEST,
            preferred_element_type=jnp.float32,
        ),
        "rows",
        scatter_dimension=0,
        tiled=True,
    )
    responses = jnp.dot(
        recovery,
        lax.all_gather(modal_rows, "rows", axis=0, tiled=True),
        precision=lax.Precision.HIGHEST,
        preferred_element_type=jnp.float32,
    )
    return finish(responses)


PLANES, SIDES = 4, 2


def index(z, y, c):
    return (z * SIDES + y) * CORES + c


def pairs_of(move):
    everyone = [(z, y, c) for z in range(PLANES) for y in range(SIDES) for c in range(CORES)]
    return [(index(*place), index(*move(*place))) for place in everyone if move(*place) is not None]


OTHER_CORE = pairs_of(lambda z, y, c: (z, y, 1 - c))
OTHER_SIDE = pairs_of(lambda z, y, c: (z, 1 - y, c))
OTHER_BOTH = pairs_of(lambda z, y, c: (z, 1 - y, 1 - c))
HOPS = [
    pairs_of(lambda z, y, c: (z ^ 1, y, c) if z in (0, 3) else None),
    pairs_of(lambda z, y, c: (3 - z, y, c) if z in (1, 2) else None),
    pairs_of(lambda z, y, c: (z ^ 1, y, c) if z in (1, 2) else None),
    OTHER_SIDE,
]


def send(value, pairs):
    return lax.ppermute(value, "rows", pairs)


def shards(histories, modal_map, recovery):
    modes = modal_map.shape[1]
    per_core = modes // CORES
    per_lane = per_core // SIDES
    place = lax.axis_index("rows")
    core, side, z = place % CORES, (place // CORES) % SIDES, place // (CORES * SIDES)
    outer = ((z == 0) | (z == PLANES - 1)).astype(jnp.int32).reshape(1)

    sizes = [part * (per_lane // 16) for part in PARTS]
    offsets = [sum(sizes[:k]) for k in range(len(sizes))]
    spans = [(offsets[group[0]], sum(sizes[i] for i in group)) for group in GROUPS]
    group_of = {i: g for g, group in enumerate(GROUPS) for i in group}

    lanes = [(core, side), (core, 1 - side), (1 - core, side), (1 - core, 1 - side)]
    at = jnp.stack([c * per_core + s * per_lane for c, s in lanes]).astype(jnp.int32)
    own = [core * per_core + side * per_lane, core * per_core + (1 - side) * per_lane]
    their = [side * per_lane, (1 - side) * per_lane]
    recovery_at = jnp.stack(own + their).astype(jnp.int32)
    other_half = ((1 - core) * per_core).astype(jnp.int32).reshape(1)

    cuts = [(2, 0, per_lane)] + [(k, *span) for span in spans for k in (1, 3)]
    pieces = list(cut(modal_map, at, cuts))
    map_from_core = send(pieces[0], OTHER_CORE)
    side_histories = send(histories, OTHER_SIDE)
    pieces = [pieces[1 + 2 * g : 3 + 2 * g] for g in range(len(GROUPS))]
    maps, held, flying = {}, {}, {}
    total, after, recovery_got, plane_histories = None, [], None, None
    for work in ORDER.split():
        if work[0] == "m":
            g = int(work[1:])
            if g == 1:
                joined = list(join([histories, side_histories], pieces[g], [map_from_core] + maps[0]))
                pieces[g] = joined[1:]
                plane_histories = [joined[0], send(joined[0], OTHER_CORE)]
                after = joined[:1]
            maps[g] = [send(piece, pairs) for piece, pairs in zip(pieces[g], [OTHER_SIDE, OTHER_BOTH])]
            continue
        if work == "rs":
            after = list(cut(recovery, other_half, [(0, 0, per_core)], after))
            recovery_got = send(after[0], OTHER_CORE)
            continue
        if work == "rw":
            after = after + [recovery_got]
            continue
        i, step = (int(part) for part in work.split("."))
        if step == 0:
            side_map, both_map = maps[group_of[i]]
            begin = offsets[i] - spans[group_of[i]][0]
            value = plane_sum(
                at, modal_map, [side_map, map_from_core, both_map], plane_histories,
                offsets[i], [begin, offsets[i], begin], sizes[i], after,
            )
        elif step <= 2:
            value = add(held[i], flying[i], after)
        elif step == 3:
            value = choose(outer, held[i], flying[i], held[i - 1] if i - 1 in JOINED else None, after)
        elif i in JOINED:
            continue
        else:
            first = i - 1 if i - 1 in JOINED else i
            parts = [held[i], flying[i]]
            value = total = recover(recovery_at, recovery, recovery_got, offsets[first], parts, total, after)
        after = [value]
        if step < 4:
            held[i] = value
            if step < 3 or i not in JOINED:
                flying[i] = send(value, HOPS[step])

    rows = recovery.shape[0]
    return finish(total[:rows] + send(total[rows:], OTHER_CORE))


def solution(mesh):
    return jax.shard_map(
        shards if (mesh.shape["grp"], mesh.shape["rows"]) == (2, 16) else plain,
        mesh=mesh,
        in_specs=(P(("grp", "rows"), None), P(("grp", "rows"), None), P(("grp", "rows"), None)),
        out_specs=(P(("grp", "rows"), None), P(None, ("grp", "rows")), P(None, ("grp", "rows"))),
        check_vma=False,
    )
```

```python
import jax
import jax.numpy as jnp
from jax import lax
from jax.experimental import pallas as pl
from jax.experimental.pallas import tpu as pltpu
from jax.sharding import PartitionSpec as P

CASES = 4
CORES = 2
PARTS = [2, 2, 2, 2, 2, 2, 2, 2]
GROUPS = [[0], [1, 2], [3, 4, 5, 6, 7]]
COSTS = [500000000, 500000000, 500000000, 1, 1, 500000000, 2000000000, 100000000000]
SEND_RECOVERY, WAIT_RECOVERY = 100, 101
ORDER = [-1, -2, 0, 10, 1, 100, 11, 20, -3, 101, 2, 21, 12, 3, 30, 40, 22, 13, 4, 31, 50, 23, 14, 41, 32, 60, 24, 51, 42, 33, 61, 70, 52, 43, 34, 62, 71, 53, 44, 63, 72, 54, 64, 73, 74]

epsilon = 1e-06

VMEM = pl.BlockSpec(memory_space=pltpu.VMEM)
ANYWHERE = pl.BlockSpec(memory_space=pl.ANY)


SCALARS = pl.BlockSpec(memory_space=pltpu.SMEM)
PARAMS = pltpu.CompilerParams(vmem_limit_bytes=16 * 1024 * 1024)


def cost(kind):
    return pl.CostEstimate(flops=COSTS[kind], bytes_accessed=1, transcendentals=0)


def halves(value):
    high = value.astype(jnp.bfloat16)
    return high, (value - high.astype(jnp.float32)).astype(jnp.bfloat16)


def dot(a, b, a_dim):
    a_high, a_low = halves(a)
    b_high, b_low = halves(b)

    def product(x, y):
        return lax.dot_general(x, y, (((a_dim,), (0,)), ((), ())), preferred_element_type=jnp.float32)

    return product(a_high, b_high) + (product(a_high, b_low) + product(a_low, b_high))


def cut_kernel(cuts, at_ref, source, *refs):
    outs, sems = refs[: len(cuts)], refs[len(cuts)]
    copies = []
    for k, (which, begin, size) in enumerate(cuts):
        column = pl.multiple_of(at_ref[which] + begin, 128)
        copies.append(pltpu.make_async_copy(source.at[:, pl.ds(column, size)], outs[k], sems.at[k]))
        copies[-1].start()
    for copy in copies:
        copy.wait()


def cut(source, at, cuts, after=(), kind=5):
    def kernel(at_ref, source_ref, *refs):
        cut_kernel(cuts, at_ref, source_ref, *refs[len(after) :])

    return pl.pallas_call(
        kernel,
        out_shape=[jax.ShapeDtypeStruct((source.shape[0], size), source.dtype) for _, _, size in cuts],
        in_specs=[SCALARS, ANYWHERE] + [ANYWHERE] * len(after),
        out_specs=[ANYWHERE] * len(cuts),
        scratch_shapes=[pltpu.SemaphoreType.DMA((len(cuts),))],
        cost_estimate=cost(kind),
        compiler_params=PARAMS,
        name="cut_columns",
    )(at, source, *after)


def join(parts, passed, after):
    rows = sum(part.shape[0] for part in parts)
    count = len(parts)

    def kernel(*refs):
        out = refs[count + len(passed) + len(after)]
        begin = 0
        for ref in refs[:count]:
            out[begin : begin + ref.shape[0]] = ref[...]
            begin += ref.shape[0]

    return pl.pallas_call(
        kernel,
        out_shape=[jax.ShapeDtypeStruct((rows, parts[0].shape[1]), jnp.float32)]
        + [jax.ShapeDtypeStruct(piece.shape, piece.dtype) for piece in passed],
        in_specs=[VMEM] * count + [ANYWHERE] * (len(passed) + len(after)),
        out_specs=[VMEM] + [ANYWHERE] * len(passed),
        input_output_aliases={count + k: 1 + k for k in range(len(passed))},
        cost_estimate=cost(6),
        compiler_params=PARAMS,
        name="join",
    )(*parts, *passed, *after)


def plane_sum(at, modal_map, maps, histories, begin, past, size, after):
    count = len(maps) + 1
    pairs = len(histories)
    depth, width = modal_map.shape[0], histories[0].shape[1]

    def kernel(at_ref, *refs):
        sources, history_refs = refs[:count], refs[count : count + pairs]
        out, block, sems = refs[-3:]
        copies = []
        for k in range(count):
            if k == 0:
                source = sources[0].at[:, pl.ds(pl.multiple_of(at_ref[0] + begin, 128), size)]
            else:
                source = sources[k].at[:, pl.ds(past[k - 1], size)]
            copies.append(pltpu.make_async_copy(source, block.at[pl.ds(k * depth, depth)], sems.at[k]))
            copies[-1].start()
        past_block = jnp.concatenate([ref[...] for ref in history_refs])
        for copy in copies:
            copy.wait()
        out[...] = dot(block[...], past_block, 0)

    return pl.pallas_call(
        kernel,
        out_shape=jax.ShapeDtypeStruct((size, width), jnp.float32),
        in_specs=[SCALARS, ANYWHERE]
        + [ANYWHERE] * len(maps)
        + [VMEM] * pairs
        + [ANYWHERE] * len(after),
        out_specs=VMEM,
        scratch_shapes=[
            pltpu.VMEM((count * depth, size), jnp.float32),
            pltpu.SemaphoreType.DMA((count,)),
        ],
        cost_estimate=cost(0),
        compiler_params=PARAMS,
        name="plane_sum",
    )(at, modal_map, *maps, *histories, *after)


def add(held, got, after):
    def kernel(held_ref, got_ref, *refs):
        refs[-1][...] = held_ref[...] + got_ref[...]

    return pl.pallas_call(
        kernel,
        out_shape=jax.ShapeDtypeStruct(held.shape, held.dtype),
        in_specs=[VMEM, VMEM] + [ANYWHERE] * len(after),
        out_specs=VMEM,
        cost_estimate=cost(1),
        compiler_params=PARAMS,
        name="add",
    )(held, got, *after)


def choose(takes, held, got, after):
    def kernel(takes_ref, held_ref, got_ref, *refs):
        out = refs[-1]

        @pl.when(takes_ref[0] == 1)
        def _():
            out[...] = got_ref[...]

        @pl.when(takes_ref[0] == 0)
        def _():
            out[...] = held_ref[...]

    return pl.pallas_call(
        kernel,
        out_shape=jax.ShapeDtypeStruct(held.shape, held.dtype),
        in_specs=[SCALARS, VMEM, VMEM] + [ANYWHERE] * len(after),
        out_specs=VMEM,
        cost_estimate=cost(3),
        compiler_params=PARAMS,
        name="choose",
    )(takes, held, got, *after)


def recover(at, recovery, recovery_got, begin, parts, total, after):
    size = parts[0].shape[0]
    count = len(parts)
    mine = recovery.shape[0]
    has_total = total is not None
    sources = count * 2

    def kernel(at_ref, recovery_ref, got_ref, *refs):
        parts_refs = refs[:count]
        total_ref = refs[count] if has_total else None
        out, block, sems = refs[-3:]
        copies = []
        for k in range(count):
            for j, source in enumerate((recovery_ref, got_ref)):
                column = pl.multiple_of(at_ref[j * count + k] + begin, 128)
                copies.append(
                    pltpu.make_async_copy(
                        source.at[:, pl.ds(column, size)],
                        block.at[pl.ds(j * mine, mine), pl.ds(k * size, size)],
                        sems.at[2 * k + j],
                    )
                )
                copies[-1].start()
        part = jnp.concatenate([ref[...] for ref in parts_refs])
        for copy in copies:
            copy.wait()
        value = dot(block[...], part, 1)
        out[...] = value + total_ref[...] if has_total else value

    rows, columns = 2 * mine, parts[0].shape[1]
    return pl.pallas_call(
        kernel,
        out_shape=jax.ShapeDtypeStruct((rows, columns), jnp.float32),
        in_specs=[SCALARS, ANYWHERE, ANYWHERE]
        + [VMEM] * count
        + [VMEM] * has_total
        + [ANYWHERE] * len(after),
        out_specs=VMEM,
        scratch_shapes=[pltpu.VMEM((rows, count * size), jnp.float32), pltpu.SemaphoreType.DMA((sources,))],
        cost_estimate=cost(4),
        compiler_params=PARAMS,
        name="recover",
    )(at, recovery, recovery_got, *parts, *([total] if has_total else []), *after)


def finish(responses):
    by_case = responses.reshape(responses.shape[0], CASES, responses.shape[1] // CASES)
    peak_response = jnp.max(jnp.abs(by_case), axis=2).T
    rms_response = jnp.sqrt(jnp.mean(by_case * by_case, axis=2) + epsilon).T
    return (responses, peak_response, rms_response)


def plain(histories, modal_map, recovery):
    modal_rows = lax.psum_scatter(
        lax.dot_general(
            modal_map,
            histories,
            (((0,), (0,)), ((), ())),
            precision=lax.Precision.HIGHEST,
            preferred_element_type=jnp.float32,
        ),
        "rows",
        scatter_dimension=0,
        tiled=True,
    )
    responses = jnp.dot(
        recovery,
        lax.all_gather(modal_rows, "rows", axis=0, tiled=True),
        precision=lax.Precision.HIGHEST,
        preferred_element_type=jnp.float32,
    )
    return finish(responses)


PLANES, SIDES = 4, 2


def index(z, y, c):
    return (z * SIDES + y) * CORES + c


def pairs_of(move):
    everyone = [(z, y, c) for z in range(PLANES) for y in range(SIDES) for c in range(CORES)]
    return [(index(*place), index(*move(*place))) for place in everyone if move(*place) is not None]


OTHER_CORE = pairs_of(lambda z, y, c: (z, y, 1 - c))
OTHER_SIDE = pairs_of(lambda z, y, c: (z, 1 - y, c))
OTHER_BOTH = pairs_of(lambda z, y, c: (z, 1 - y, 1 - c))
HOPS = [
    pairs_of(lambda z, y, c: (z ^ 1, y, c) if z in (0, 3) else None),
    pairs_of(lambda z, y, c: (3 - z, y, c) if z in (1, 2) else None),
    pairs_of(lambda z, y, c: (z ^ 1, y, c) if z in (1, 2) else None),
    OTHER_SIDE,
]


def send(value, pairs):
    return lax.ppermute(value, "rows", pairs)


def shards(histories, modal_map, recovery):
    modes = modal_map.shape[1]
    per_core = modes // CORES
    per_lane = per_core // SIDES
    place = lax.axis_index("rows")
    core, side, z = place % CORES, (place // CORES) % SIDES, place // (CORES * SIDES)
    outer = ((z == 0) | (z == PLANES - 1)).astype(jnp.int32).reshape(1)

    sizes = [part * (per_lane // 16) for part in PARTS]
    offsets = [sum(sizes[:k]) for k in range(len(sizes))]
    spans = [(offsets[group[0]], sum(sizes[i] for i in group)) for group in GROUPS]
    group_of = {i: g for g, group in enumerate(GROUPS) for i in group}

    lanes = [(core, side), (core, 1 - side), (1 - core, side), (1 - core, 1 - side)]
    at = jnp.stack([c * per_core + s * per_lane for c, s in lanes]).astype(jnp.int32)
    own = [core * per_core + side * per_lane, core * per_core + (1 - side) * per_lane]
    their = [side * per_lane, (1 - side) * per_lane]
    recovery_at = jnp.stack(own + their).astype(jnp.int32)
    other_half = ((1 - core) * per_core).astype(jnp.int32).reshape(1)

    cuts = [(2, 0, per_lane)] + [(k, *span) for span in spans for k in (1, 3)]
    pieces = list(cut(modal_map, at, cuts, kind=7))
    map_from_core = send(pieces[0], OTHER_CORE)
    side_histories = send(histories, OTHER_SIDE)
    pieces = [pieces[1 + 2 * g : 3 + 2 * g] for g in range(len(GROUPS))]
    maps, held, flying = {}, {}, {}
    total, after, recovery_got, plane_histories = None, [], None, None
    for work in ORDER:
        if work < 0:
            g = -1 - work
            if g == 1:
                joined = list(join([histories, side_histories], pieces[g], [map_from_core] + maps[0]))
                pieces[g] = joined[1:]
                plane_histories = [joined[0], send(joined[0], OTHER_CORE)]
                after = joined[:1]
            maps[g] = [send(piece, pairs) for piece, pairs in zip(pieces[g], [OTHER_SIDE, OTHER_BOTH])]
            continue
        if work == SEND_RECOVERY:
            after = list(cut(recovery, other_half, [(0, 0, per_core)], after))
            recovery_got = send(after[0], OTHER_CORE)
            continue
        if work == WAIT_RECOVERY:
            after = after + [recovery_got]
            continue
        i, step = divmod(work, 10)
        if step == 0:
            side_map, both_map = maps[group_of[i]]
            begin = offsets[i] - spans[group_of[i]][0]
            value = plane_sum(
                at, modal_map, [side_map, map_from_core, both_map], plane_histories,
                offsets[i], [begin, offsets[i], begin], sizes[i], after,
            )
        elif step <= 2:
            value = add(held[i], flying[i], after)
        elif step == 3:
            value = choose(outer, held[i], flying[i], after)
        else:
            parts = [held[i], flying[i]]
            value = total = recover(recovery_at, recovery, recovery_got, offsets[i], parts, total, after)
        after = [value]
        if step < 4:
            held[i] = value
            flying[i] = send(value, HOPS[step])

    rows = recovery.shape[0]
    return finish(total[:rows] + send(total[rows:], OTHER_CORE))


def solution(mesh):
    return jax.shard_map(
        shards if (mesh.shape["grp"], mesh.shape["rows"]) == (2, 16) else plain,
        mesh=mesh,
        in_specs=(P(("grp", "rows"), None), P(("grp", "rows"), None), P(("grp", "rows"), None)),
        out_specs=(P(("grp", "rows"), None), P(None, ("grp", "rows")), P(None, ("grp", "rows"))),
        check_vma=False,
    )
```

```python
import jax
import jax.numpy as jnp
from jax import lax
from jax.experimental import pallas as pl
from jax.experimental.pallas import tpu as pltpu
from jax.sharding import PartitionSpec as P

CASES = 4
CORES = 2
PARTS = [2, 2, 2, 2, 2, 2, 2, 2]
GROUPS = [[0], [1, 2], [3, 4, 5, 6, 7]]
COSTS = {-1: 100000000000, -2: 2000000000, 0: 2000000000, 10: 20000000000, 3: 1, 4: 1, 13: 1, 14: 1, 23: 1, 24: 1, 33: 1, 34: 1, 43: 5000000000, 44: 1, 53: 1, 54: 1, 63: 1, 64: 1, 73: 1, 74: 1, 20: 20000000000, 11: 20000000000}
SEND_RECOVERY, WAIT_RECOVERY = 100, 101
ORDER = [-1, -2, 0, 10, 1, 100, 11, 20, -3, 101, 2, 21, 12, 3, 30, 40, 22, 13, 4, 31, 50, 23, 14, 41, 32, 60, 24, 51, 42, 33, 61, 70, 52, 43, 34, 62, 71, 53, 44, 63, 72, 54, 64, 73, 74]

epsilon = 1e-06

VMEM = pl.BlockSpec(memory_space=pltpu.VMEM)
ANYWHERE = pl.BlockSpec(memory_space=pl.ANY)


SCALARS = pl.BlockSpec(memory_space=pltpu.SMEM)
PARAMS = pltpu.CompilerParams(vmem_limit_bytes=16 * 1024 * 1024)


def cost(kind):
    return pl.CostEstimate(flops=COSTS.get(kind, 500000000), bytes_accessed=1, transcendentals=0)


def halves(value):
    high = value.astype(jnp.bfloat16)
    return high, (value - high.astype(jnp.float32)).astype(jnp.bfloat16)


def dot(a, b, a_dim):
    a_high, a_low = halves(a)
    b_high, b_low = halves(b)

    def product(x, y):
        return lax.dot_general(x, y, (((a_dim,), (0,)), ((), ())), preferred_element_type=jnp.float32)

    return product(a_high, b_high) + (product(a_high, b_low) + product(a_low, b_high))


def cut_kernel(cuts, at_ref, source, *refs):
    outs, sems = refs[: len(cuts)], refs[len(cuts)]
    copies = []
    for k, (which, begin, size) in enumerate(cuts):
        column = pl.multiple_of(at_ref[which] + begin, 128)
        copies.append(pltpu.make_async_copy(source.at[:, pl.ds(column, size)], outs[k], sems.at[k]))
        copies[-1].start()
    for copy in copies:
        copy.wait()


def cut(source, at, cuts, after=(), kind=SEND_RECOVERY):
    def kernel(at_ref, source_ref, *refs):
        cut_kernel(cuts, at_ref, source_ref, *refs[len(after) :])

    return pl.pallas_call(
        kernel,
        out_shape=[jax.ShapeDtypeStruct((source.shape[0], size), source.dtype) for _, _, size in cuts],
        in_specs=[SCALARS, ANYWHERE] + [ANYWHERE] * len(after),
        out_specs=[ANYWHERE] * len(cuts),
        scratch_shapes=[pltpu.SemaphoreType.DMA((len(cuts),))],
        cost_estimate=cost(kind),
        compiler_params=PARAMS,
        name="cut_columns",
    )(at, source, *after)


def join(parts, passed, after):
    rows = sum(part.shape[0] for part in parts)
    count = len(parts)

    def kernel(*refs):
        out = refs[count + len(passed) + len(after)]
        begin = 0
        for ref in refs[:count]:
            out[begin : begin + ref.shape[0]] = ref[...]
            begin += ref.shape[0]

    return pl.pallas_call(
        kernel,
        out_shape=[jax.ShapeDtypeStruct((rows, parts[0].shape[1]), jnp.float32)]
        + [jax.ShapeDtypeStruct(piece.shape, piece.dtype) for piece in passed],
        in_specs=[VMEM] * count + [ANYWHERE] * (len(passed) + len(after)),
        out_specs=[VMEM] + [ANYWHERE] * len(passed),
        input_output_aliases={count + k: 1 + k for k in range(len(passed))},
        cost_estimate=cost(-2),
        compiler_params=PARAMS,
        name="join",
    )(*parts, *passed, *after)


def plane_sum(at, modal_map, maps, histories, begin, past, size, work, after):
    count = len(maps) + 1
    pairs = len(histories)
    depth, width = modal_map.shape[0], histories[0].shape[1]

    def kernel(at_ref, *refs):
        sources, history_refs = refs[:count], refs[count : count + pairs]
        out, block, sems = refs[-3:]
        copies = []
        for k in range(count):
            if k == 0:
                source = sources[0].at[:, pl.ds(pl.multiple_of(at_ref[0] + begin, 128), size)]
            else:
                source = sources[k].at[:, pl.ds(past[k - 1], size)]
            copies.append(pltpu.make_async_copy(source, block.at[pl.ds(k * depth, depth)], sems.at[k]))
            copies[-1].start()
        past_block = jnp.concatenate([ref[...] for ref in history_refs])
        for copy in copies:
            copy.wait()
        out[...] = dot(block[...], past_block, 0)

    return pl.pallas_call(
        kernel,
        out_shape=jax.ShapeDtypeStruct((size, width), jnp.float32),
        in_specs=[SCALARS, ANYWHERE]
        + [ANYWHERE] * len(maps)
        + [VMEM] * pairs
        + [ANYWHERE] * len(after),
        out_specs=VMEM,
        scratch_shapes=[
            pltpu.VMEM((count * depth, size), jnp.float32),
            pltpu.SemaphoreType.DMA((count,)),
        ],
        cost_estimate=cost(work),
        compiler_params=PARAMS,
        name="plane_sum",
    )(at, modal_map, *maps, *histories, *after)


def add(held, got, work, after):
    def kernel(held_ref, got_ref, *refs):
        refs[-1][...] = held_ref[...] + got_ref[...]

    return pl.pallas_call(
        kernel,
        out_shape=jax.ShapeDtypeStruct(held.shape, held.dtype),
        in_specs=[VMEM, VMEM] + [ANYWHERE] * len(after),
        out_specs=VMEM,
        cost_estimate=cost(work),
        compiler_params=PARAMS,
        name="add",
    )(held, got, *after)


def choose(takes, held, got, work, after):
    def kernel(takes_ref, held_ref, got_ref, *refs):
        out = refs[-1]

        @pl.when(takes_ref[0] == 1)
        def _():
            out[...] = got_ref[...]

        @pl.when(takes_ref[0] == 0)
        def _():
            out[...] = held_ref[...]

    return pl.pallas_call(
        kernel,
        out_shape=jax.ShapeDtypeStruct(held.shape, held.dtype),
        in_specs=[SCALARS, VMEM, VMEM] + [ANYWHERE] * len(after),
        out_specs=VMEM,
        cost_estimate=cost(work),
        compiler_params=PARAMS,
        name="choose",
    )(takes, held, got, *after)


def recover(at, recovery, recovery_got, begin, parts, total, work, after):
    size = parts[0].shape[0]
    count = len(parts)
    mine = recovery.shape[0]
    has_total = total is not None
    sources = count * 2

    def kernel(at_ref, recovery_ref, got_ref, *refs):
        parts_refs = refs[:count]
        total_ref = refs[count] if has_total else None
        out, block, sems = refs[-3:]
        copies = []
        for k in range(count):
            for j, source in enumerate((recovery_ref, got_ref)):
                column = pl.multiple_of(at_ref[j * count + k] + begin, 128)
                copies.append(
                    pltpu.make_async_copy(
                        source.at[:, pl.ds(column, size)],
                        block.at[pl.ds(j * mine, mine), pl.ds(k * size, size)],
                        sems.at[2 * k + j],
                    )
                )
                copies[-1].start()
        part = jnp.concatenate([ref[...] for ref in parts_refs])
        for copy in copies:
            copy.wait()
        value = dot(block[...], part, 1)
        out[...] = value + total_ref[...] if has_total else value

    rows, columns = 2 * mine, parts[0].shape[1]
    return pl.pallas_call(
        kernel,
        out_shape=jax.ShapeDtypeStruct((rows, columns), jnp.float32),
        in_specs=[SCALARS, ANYWHERE, ANYWHERE]
        + [VMEM] * count
        + [VMEM] * has_total
        + [ANYWHERE] * len(after),
        out_specs=VMEM,
        scratch_shapes=[pltpu.VMEM((rows, count * size), jnp.float32), pltpu.SemaphoreType.DMA((sources,))],
        cost_estimate=cost(work),
        compiler_params=PARAMS,
        name="recover",
    )(at, recovery, recovery_got, *parts, *([total] if has_total else []), *after)


def finish(responses):
    by_case = responses.reshape(responses.shape[0], CASES, responses.shape[1] // CASES)
    peak_response = jnp.max(jnp.abs(by_case), axis=2).T
    rms_response = jnp.sqrt(jnp.mean(by_case * by_case, axis=2) + epsilon).T
    return (responses, peak_response, rms_response)


def plain(histories, modal_map, recovery):
    modal_rows = lax.psum_scatter(
        lax.dot_general(
            modal_map,
            histories,
            (((0,), (0,)), ((), ())),
            precision=lax.Precision.HIGHEST,
            preferred_element_type=jnp.float32,
        ),
        "rows",
        scatter_dimension=0,
        tiled=True,
    )
    responses = jnp.dot(
        recovery,
        lax.all_gather(modal_rows, "rows", axis=0, tiled=True),
        precision=lax.Precision.HIGHEST,
        preferred_element_type=jnp.float32,
    )
    return finish(responses)


PLANES, SIDES = 4, 2


def index(z, y, c):
    return (z * SIDES + y) * CORES + c


def pairs_of(move):
    everyone = [(z, y, c) for z in range(PLANES) for y in range(SIDES) for c in range(CORES)]
    return [(index(*place), index(*move(*place))) for place in everyone if move(*place) is not None]


OTHER_CORE = pairs_of(lambda z, y, c: (z, y, 1 - c))
OTHER_SIDE = pairs_of(lambda z, y, c: (z, 1 - y, c))
OTHER_BOTH = pairs_of(lambda z, y, c: (z, 1 - y, 1 - c))
HOPS = [
    pairs_of(lambda z, y, c: (z ^ 1, y, c) if z in (0, 3) else None),
    pairs_of(lambda z, y, c: (3 - z, y, c) if z in (1, 2) else None),
    pairs_of(lambda z, y, c: (z ^ 1, y, c) if z in (1, 2) else None),
    OTHER_SIDE,
]


def send(value, pairs):
    return lax.ppermute(value, "rows", pairs)


def shards(histories, modal_map, recovery):
    modes = modal_map.shape[1]
    per_core = modes // CORES
    per_lane = per_core // SIDES
    place = lax.axis_index("rows")
    core, side, z = place % CORES, (place // CORES) % SIDES, place // (CORES * SIDES)
    outer = ((z == 0) | (z == PLANES - 1)).astype(jnp.int32).reshape(1)

    sizes = [part * (per_lane // 16) for part in PARTS]
    offsets = [sum(sizes[:k]) for k in range(len(sizes))]
    spans = [(offsets[group[0]], sum(sizes[i] for i in group)) for group in GROUPS]
    group_of = {i: g for g, group in enumerate(GROUPS) for i in group}

    lanes = [(core, side), (core, 1 - side), (1 - core, side), (1 - core, 1 - side)]
    at = jnp.stack([c * per_core + s * per_lane for c, s in lanes]).astype(jnp.int32)
    own = [core * per_core + side * per_lane, core * per_core + (1 - side) * per_lane]
    their = [side * per_lane, (1 - side) * per_lane]
    recovery_at = jnp.stack(own + their).astype(jnp.int32)
    other_half = ((1 - core) * per_core).astype(jnp.int32).reshape(1)

    cuts = [(2, 0, per_lane)] + [(k, *span) for span in spans for k in (1, 3)]
    pieces = list(cut(modal_map, at, cuts, kind=-1))
    map_from_core = send(pieces[0], OTHER_CORE)
    side_histories = send(histories, OTHER_SIDE)
    pieces = [pieces[1 + 2 * g : 3 + 2 * g] for g in range(len(GROUPS))]
    maps, held, flying = {}, {}, {}
    total, after, recovery_got, plane_histories = None, [], None, None
    for work in ORDER:
        if work < 0:
            g = -1 - work
            if g == 1:
                joined = list(join([histories, side_histories], pieces[g], [map_from_core] + maps[0]))
                pieces[g] = joined[1:]
                plane_histories = [joined[0], send(joined[0], OTHER_CORE)]
                after = joined[:1]
            maps[g] = [send(piece, pairs) for piece, pairs in zip(pieces[g], [OTHER_SIDE, OTHER_BOTH])]
            continue
        if work == SEND_RECOVERY:
            after = list(cut(recovery, other_half, [(0, 0, per_core)], after))
            recovery_got = send(after[0], OTHER_CORE)
            continue
        if work == WAIT_RECOVERY:
            after = after + [recovery_got]
            continue
        i, step = divmod(work, 10)
        if step == 0:
            side_map, both_map = maps[group_of[i]]
            begin = offsets[i] - spans[group_of[i]][0]
            value = plane_sum(
                at, modal_map, [side_map, map_from_core, both_map], plane_histories,
                offsets[i], [begin, offsets[i], begin], sizes[i], work, after,
            )
        elif step <= 2:
            value = add(held[i], flying[i], work, after)
        elif step == 3:
            value = choose(outer, held[i], flying[i], work, after)
        else:
            parts = [held[i], flying[i]]
            value = total = recover(recovery_at, recovery, recovery_got, offsets[i], parts, total, work, after)
        after = [value]
        if step < 4:
            held[i] = value
            flying[i] = send(value, HOPS[step])

    rows = recovery.shape[0]
    return finish(total[:rows] + send(total[rows:], OTHER_CORE))


def solution(mesh):
    return jax.shard_map(
        shards if (mesh.shape["grp"], mesh.shape["rows"]) == (2, 16) else plain,
        mesh=mesh,
        in_specs=(P(("grp", "rows"), None), P(("grp", "rows"), None), P(("grp", "rows"), None)),
        out_specs=(P(("grp", "rows"), None), P(None, ("grp", "rows")), P(None, ("grp", "rows"))),
        check_vma=False,
    )
```
